512 devices in a mesh: tm: 128 (over z_hi, x, y), rows: 4 (over z_lo, core).
Axes of the slice: x: 4, y: 8, z: 8 (z_hi: 4, z_lo: 2; z = z_hi * 2 + z_lo), core: 2. Of those that a mesh axis runs over, the one named last changes fastest.
Arguments:
- stream: bfloat16 [512, 32, 96, 128], P('tm', 'rows'), may hold values from -6 to 6
- gains: float32 [2, 96], replicated, may hold values from 0.5 to 2
- kernels: bfloat16 [2, 3, 3, 3, 96, 96], replicated, may hold values from -0.125 to 0.125
- biases: float32 [2, 96], replicated, may hold values from -3 to 3
Outputs:
- decoded: bfloat16 [512, 32, 96, 128], P('tm', 'rows')
The draws below stay inside these ranges and needn't reach their ends.
All inputs are finite; a program needn't handle non-finite values.
Results may differ from the reference program's by a relative error of at most 0.0039.
Values may be sent and summed in bfloat16 or wider, within the bound.
No kernel may reach another device: no remote copies, remote signals or barrier semaphores. Data moves between devices by JAX's collectives and lax.ppermute only.
A program may use at most 64 MiB of HBM per device.

```python
import math
import jax
import jax.numpy as jnp
from jax import lax

C = 96
CONVS = 2
W = 128
NF = 512
NR = 32


def level_of(key, extent, pieces, smallest, largest):
    level, own = 1.0, jax.random.fold_in(key, 6)
    for axis_at, blocks in pieces:
        heights = jnp.exp(jax.random.uniform(jax.random.fold_in(own, axis_at), (blocks,), jnp.float32, smallest / len(pieces), largest / len(pieces)))
        level = level * jnp.repeat(heights, extent[axis_at] // blocks).reshape([-1 if axis == axis_at else 1 for axis in range(len(extent))])
    return level


def gaussian(key, extent, width, most, cuts=(), kind=jnp.bfloat16):
    values = width * jax.random.normal(key, extent, jnp.float32)
    if cuts:
        values = values * level_of(key, extent, cuts, -0.22, 0.18)
    return jnp.clip(values, -most, most).astype(kind)


def setup_inputs(seed: int = 0) -> dict:
    streams_of = jax.random.split(jax.random.key(seed), 5)
    return {
        "stream": gaussian(streams_of[0], (NF, NR, C, W), 1.0, 6.0, ((0, 128), (1, 4))),
        "gains": jnp.clip(jnp.exp(jax.random.uniform(streams_of[1], (CONVS, C), jnp.float32, math.log(0.5), math.log(2.0))), 0.5, 2.0),
        "kernels": gaussian(streams_of[2], (CONVS, 3, 3, 3, C, C), (27 * C) ** -0.5, 0.125),
        "biases": gaussian(streams_of[3], (CONVS, C), 0.5, 3.0, (), jnp.float32),
    }


EPS = 1e-06

def channel_norm(values, gain):
    floats = values.astype(jnp.float32)
    mean_sq = lax.optimization_barrier(jnp.mean(floats * floats, axis=2, keepdims=True))
    scaled = floats * lax.rsqrt(mean_sq + EPS) * gain.astype(jnp.float32)[None, None, :, None]
    return jax.nn.silu(scaled).astype(jnp.bfloat16)

def causal_conv(normed, kernel, bias):
    inputs = jnp.transpose(normed.astype(jnp.float32), (0, 1, 3, 2))[None]
    result = lax.conv_general_dilated(inputs, kernel.astype(jnp.float32), (1, 1, 1), [(2, 0), (1, 1), (1, 1)], dimension_numbers=('NDHWC', 'DHWIO', 'NDHWC'), precision=lax.Precision.HIGHEST)
    return jnp.transpose(result[0], (0, 1, 3, 2)) + bias.astype(jnp.float32)[None, None, :, None]

def reference(stream, gains, kernels, biases):
    current = stream
    for section in range(CONVS // 2):
        first = 2 * section
        hidden = causal_conv(channel_norm(current, gains[first]), kernels[first], biases[first])
        branch = causal_conv(channel_norm(hidden, gains[first + 1]), kernels[first + 1], biases[first + 1])
        current = (current.astype(jnp.float32) + branch).astype(jnp.bfloat16)
    return current
```

```python
import functools

import jax
import jax.numpy as jnp
from jax import lax
from jax.experimental import pallas as pl
from jax.experimental.pallas import tpu as pltpu
from jax.sharding import PartitionSpec as P

EPS = 1e-06
VMEM_BYTES = 48 * 1024 * 1024
F32 = jnp.float32
BF16 = jnp.bfloat16


def activated(values, gain):
    mean_sq = jnp.mean(values * values, axis=0, keepdims=True)
    half = values * lax.rsqrt(mean_sq + EPS) * (0.5 * gain)
    return half + half * jnp.tanh(half)


def store_taps(ref, frame, row, act):
    channels, cols = act.shape
    lane = lax.broadcasted_iota(jnp.int32, act.shape, 1)
    left = jnp.where(lane == 0, 0.0, pltpu.roll(act, 1, 1))
    right = jnp.where(lane == cols - 1, 0.0, pltpu.roll(act, cols - 1, 1))
    ref[frame, row, 0:channels] = left.astype(BF16)
    ref[frame, row, channels : 2 * channels] = act.astype(BF16)
    ref[frame, row, 2 * channels :] = right.astype(BF16)


def row_pair(ref, frame, row):
    depth, cols = ref.shape[2], ref.shape[3]
    first = ref[frame, row : row + 3].reshape(3 * depth, cols)
    second = ref[frame, row + 1 : row + 4].reshape(3 * depth, cols)
    return jnp.concatenate([first, second], axis=1)


def tap_products(weights_ref, index, taps, columns):
    channels = weights_ref.shape[1] // 3
    low, high = taps
    product = jnp.dot(
        weights_ref[index, low * channels : (high + 1) * channels],
        columns,
        preferred_element_type=F32,
    )
    return {
        tap: product[(tap - low) * channels : (tap - low + 1) * channels]
        for tap in range(low, high + 1)
    }


def prepare_kernel(kernels_ref, gains_ref, biases_ref, weights_ref, gain_ref, bias_ref):
    channels = gains_ref.shape[1]
    cols = gain_ref.shape[2]
    for index in range(2):
        for tap in range(3):
            weights_ref[index, tap * channels : (tap + 1) * channels, :] = kernels_ref[index, tap].T
        for source, target in ((gains_ref, gain_ref), (biases_ref, bias_ref)):
            spread = jnp.broadcast_to(source[index : index + 1], (cols, channels))
            target[index] = spread.T


def halves(pair):
    cols = pair.shape[1] // 2
    return pair[:, :cols], pair[:, cols:]


def local_kernel(
    stream_ref, above_ref, below_ref, weights_ref, gain_ref, bias_ref,
    send_ref, hidden_ref, base_ref,
    taps_ref, normed_ref,
):
    frames, rows = stream_ref.shape[:2]
    band = lax.axis_index("rows")
    keep_above = jnp.where(band > 0, 1.0, 0.0)
    keep_below = jnp.where(band < lax.axis_size("rows") - 1, 1.0, 0.0)
    gain = gain_ref[0]
    for frame in range(frames):
        for row in range(rows + 4):
            if row < 2:
                values = above_ref[frame, row]
            elif row < rows + 2:
                values = stream_ref[frame, row - 2]
            else:
                values = below_ref[frame, row - rows - 2]
            store_taps(taps_ref, frame, row, activated(values.astype(F32), gain))
    gain = gain_ref[1]
    bias = jnp.concatenate([bias_ref[0]] * 2, axis=1)
    for pair in range((rows + 2) // 2):
        y = [
            tap_products(weights_ref, 0, taps, row_pair(taps_ref, frame, 2 * pair))
            for frame, taps in enumerate(((0, 2), (0, 2), (1, 2), (2, 2)))
        ]
        hidden = [
            y[0][2] + bias,
            y[0][1] + y[1][2] + bias,
            y[0][0] + y[1][1] + y[2][2] + bias,
            y[1][0] + y[2][1] + y[3][2] + bias,
        ]
        for frame in range(4):
            for side, values in enumerate(halves(hidden[frame])):
                row = 2 * pair + side
                if frame < 2:
                    hidden_ref[frame, row] = values
                    continue
                act = activated(values, gain)
                if row == 0:
                    act = act * keep_above
                if row == rows + 1:
                    act = act * keep_below
                store_taps(normed_ref, frame - 2, row, act)
    bias = bias_ref[1]
    for pair in range(rows // 2):
        y2 = tap_products(weights_ref, 1, (0, 2), row_pair(normed_ref, 0, 2 * pair))
        y3 = tap_products(weights_ref, 1, (0, 2), row_pair(normed_ref, 1, 2 * pair))
        for side in range(2):
            row = 2 * pair + side
            send_ref[0, row] = (halves(y2[0])[side] + halves(y3[1])[side]).astype(BF16)
            send_ref[1, row] = halves(y3[0])[side].astype(BF16)
            base_ref[0, row] = halves(y2[2])[side] + bias + stream_ref[2, row].astype(F32)
            base_ref[1, row] = (
                halves(y2[1])[side] + halves(y3[2])[side] + bias + stream_ref[3, row].astype(F32)
            )


def history_kernel(
    earlier_ref, above_ref, below_ref, hidden_ref, base_ref, stream_ref, weights_ref, gain_ref, bias_ref,
    out_ref, first_ref,
    taps_ref, normed_ref,
):
    rows = earlier_ref.shape[1]
    band = lax.axis_index("rows")
    keep_above = jnp.where(band > 0, 1.0, 0.0)
    keep_below = jnp.where(band < lax.axis_size("rows") - 1, 1.0, 0.0)
    gain = gain_ref[0]
    for frame in range(2):
        for row in range(rows + 4):
            if row < 2:
                values = above_ref[frame, row]
            elif row < rows + 2:
                values = earlier_ref[frame, row - 2]
            else:
                values = below_ref[frame, row - rows - 2]
            store_taps(taps_ref, frame, row, activated(values.astype(F32), gain))
    gain = gain_ref[1]
    for pair in range((rows + 2) // 2):
        y0 = tap_products(weights_ref, 0, (0, 0), row_pair(taps_ref, 0, 2 * pair))
        y1 = tap_products(weights_ref, 0, (0, 1), row_pair(taps_ref, 1, 2 * pair))
        hidden = [y0[0] + y1[1], y1[0]]
        for frame in range(2):
            for side, values in enumerate(halves(hidden[frame])):
                row = 2 * pair + side
                act = activated(values + hidden_ref[frame, row], gain)
                if row == 0:
                    act = act * keep_above
                if row == rows + 1:
                    act = act * keep_below
                store_taps(normed_ref, frame, row, act)
    bias = bias_ref[1]
    for pair in range(rows // 2):
        y0 = tap_products(weights_ref, 1, (0, 2), row_pair(normed_ref, 0, 2 * pair))
        y1 = tap_products(weights_ref, 1, (0, 2), row_pair(normed_ref, 1, 2 * pair))
        for side in range(2):
            row = 2 * pair + side
            first_ref[0, row] = halves(y0[2])[side] + bias + stream_ref[0, row].astype(F32)
            first_ref[1, row] = (
                halves(y0[1])[side] + halves(y1[2])[side] + bias + stream_ref[1, row].astype(F32)
            )
            out_ref[2, row] = (
                base_ref[0, row] + halves(y0[0])[side] + halves(y1[1])[side]
            ).astype(BF16)
            out_ref[3, row] = (base_ref[1, row] + halves(y1[0])[side]).astype(BF16)


def finish_kernel(partial_ref, first_ref, _, out_ref):
    out_ref[...] = (first_ref[...] + partial_ref[...].astype(F32)).astype(BF16)


def call(kernel, outs, scratch=(), flops=0, moved=0):
    return pl.pallas_call(
        kernel,
        out_shape=[jax.ShapeDtypeStruct(*out) for out in outs],
        scratch_shapes=list(scratch),
        compiler_params=pltpu.CompilerParams(vmem_limit_bytes=VMEM_BYTES),
        cost_estimate=pl.CostEstimate(flops=flops, bytes_accessed=moved, transcendentals=0),
    )


def steps(axis, distance):
    size = lax.axis_size(axis)
    return [(i, i + distance) for i in range(size) if 0 <= i + distance < size]


def row_edges(block):
    rows = block.shape[1]
    above = lax.ppermute(block[:, rows - 2 :], "rows", steps("rows", 1))
    below = lax.ppermute(block[:, :2], "rows", steps("rows", -1))
    return above, below


def shards(stream, gains, kernels, biases):
    frames, rows, channels, cols = stream.shape
    plane = (channels, cols)
    cells = rows * cols
    mac = 2 * 9 * channels * channels
    earlier = lax.ppermute(stream[frames - 2 :], "tm", steps("tm", 1))
    above, below = row_edges(stream)
    weights, gain, bias = call(
        prepare_kernel,
        [
            ((2, 3 * channels, 9 * channels), BF16),
            ((2, *plane), F32),
            ((2, *plane), F32),
        ],
        flops=10**6,
        moved=4 * 10**6,
    )(kernels.reshape(2, 3, 9 * channels, channels), gains, biases)
    sent, hidden, base = call(
        local_kernel,
        [
            ((2, rows, *plane), BF16),
            ((2, rows + 2, *plane), F32),
            ((2, rows, *plane), F32),
        ],
        [
            pltpu.VMEM((frames, rows + 4, 3 * channels, cols), BF16),
            pltpu.VMEM((2, rows + 2, 3 * channels, cols), BF16),
        ],
        flops=mac * cells * 18,
        moved=4 * 10**6,
    )(stream, above, below, weights, gain, bias)
    partial = lax.ppermute(sent, "tm", steps("tm", 1))
    above, below = row_edges(earlier)
    out, first = call(
        history_kernel,
        [((frames, rows, *plane), BF16), ((2, rows, *plane), F32)],
        [
            pltpu.VMEM((2, rows + 4, 3 * channels, cols), BF16),
            pltpu.VMEM((2, rows + 2, 3 * channels, cols), BF16),
        ],
        flops=mac * cells * 10,
        moved=4 * 10**6,
    )(earlier, above, below, hidden, base, stream, weights, gain, bias)
    block = pl.BlockSpec((2, rows, *plane), lambda i: (0, 0, 0, 0))
    return pl.pallas_call(
        finish_kernel,
        grid=(1,),
        out_shape=jax.ShapeDtypeStruct(stream.shape, BF16),
        in_specs=[block, block, pl.BlockSpec(memory_space=pl.ANY)],
        out_specs=block,
        input_output_aliases={2: 0},
        compiler_params=pltpu.CompilerParams(vmem_limit_bytes=VMEM_BYTES),
        cost_estimate=pl.CostEstimate(flops=10**6, bytes_accessed=2 * 10**6, transcendentals=0),
    )(partial, first, out)


def solution(mesh):
    placed = (P("tm", "rows", None, None), P(), P(), P())
    return jax.shard_map(
        shards, mesh=mesh, in_specs=placed, out_specs=P("tm", "rows", None, None), check_vma=False
    )
```

```python
import functools

import jax
import jax.numpy as jnp
from jax import lax
from jax.experimental import pallas as pl
from jax.experimental.pallas import tpu as pltpu
from jax.sharding import PartitionSpec as P

EPS = 1e-06
VMEM_BYTES = 48 * 1024 * 1024
F32 = jnp.float32
BF16 = jnp.bfloat16


def activated(values, gain):
    mean_sq = jnp.mean(values * values, axis=0, keepdims=True)
    half = values * lax.rsqrt(mean_sq + EPS) * (0.5 * gain)
    return half + half * jnp.tanh(half)


def store_taps(ref, frame, row, act):
    channels, cols = act.shape
    lane = lax.broadcasted_iota(jnp.int32, act.shape, 1)
    left = jnp.where(lane == 0, 0.0, pltpu.roll(act, 1, 1))
    right = jnp.where(lane == cols - 1, 0.0, pltpu.roll(act, cols - 1, 1))
    ref[frame, row, 0:channels] = left.astype(BF16)
    ref[frame, row, channels : 2 * channels] = act.astype(BF16)
    ref[frame, row, 2 * channels :] = right.astype(BF16)


def row_pair(ref, frame, row):
    depth, cols = ref.shape[2], ref.shape[3]
    first = ref[frame, row : row + 3].reshape(3 * depth, cols)
    second = ref[frame, row + 1 : row + 4].reshape(3 * depth, cols)
    return jnp.concatenate([first, second], axis=1)


def tap_products(weights_ref, index, taps, columns):
    channels = weights_ref.shape[1] // 3
    low, high = taps
    product = jnp.dot(
        weights_ref[index, low * channels : (high + 1) * channels],
        columns,
        preferred_element_type=F32,
    )
    return {
        tap: product[(tap - low) * channels : (tap - low + 1) * channels]
        for tap in range(low, high + 1)
    }


def prepare_kernel(kernels_ref, gains_ref, biases_ref, weights_ref, gain_ref, bias_ref):
    channels = gains_ref.shape[1]
    cols = gain_ref.shape[2]
    for index in range(2):
        for tap in range(3):
            weights_ref[index, tap * channels : (tap + 1) * channels, :] = kernels_ref[index, tap].T
        for source, target in ((gains_ref, gain_ref), (biases_ref, bias_ref)):
            spread = jnp.broadcast_to(source[index : index + 1], (cols, channels))
            target[index] = spread.T


def halves(pair):
    cols = pair.shape[1] // 2
    return pair[:, :cols], pair[:, cols:]


def local_kernel(
    stream_ref, above_ref, below_ref, weights_ref, gain_ref, bias_ref,
    send_ref, hidden_ref, base_ref,
    taps_ref, normed_ref,
):
    frames, rows = stream_ref.shape[:2]
    band = lax.axis_index("rows")
    keep_above = jnp.where(band > 0, 1.0, 0.0)
    keep_below = jnp.where(band < lax.axis_size("rows") - 1, 1.0, 0.0)
    gain = gain_ref[0]
    for frame in range(frames):
        for row in range(rows + 4):
            if row < 2:
                values = above_ref[frame, row]
            elif row < rows + 2:
                values = stream_ref[frame, row - 2]
            else:
                values = below_ref[frame, row - rows - 2]
            store_taps(taps_ref, frame, row, activated(values.astype(F32), gain))
    gain = gain_ref[1]
    bias = jnp.concatenate([bias_ref[0]] * 2, axis=1)
    for pair in range((rows + 2) // 2):
        y = [
            tap_products(weights_ref, 0, taps, row_pair(taps_ref, frame, 2 * pair))
            for frame, taps in enumerate(((0, 2), (0, 2), (1, 2), (2, 2)))
        ]
        hidden = [
            y[0][2] + bias,
            y[0][1] + y[1][2] + bias,
            y[0][0] + y[1][1] + y[2][2] + bias,
            y[1][0] + y[2][1] + y[3][2] + bias,
        ]
        for frame in range(4):
            for side, values in enumerate(halves(hidden[frame])):
                row = 2 * pair + side
                if frame < 2:
                    hidden_ref[frame, row] = values
                    continue
                act = activated(values, gain)
                if row == 0:
                    act = act * keep_above
                if row == rows + 1:
                    act = act * keep_below
                store_taps(normed_ref, frame - 2, row, act)
    bias = bias_ref[1]
    for pair in range(rows // 2):
        y2 = tap_products(weights_ref, 1, (0, 2), row_pair(normed_ref, 0, 2 * pair))
        y3 = tap_products(weights_ref, 1, (0, 2), row_pair(normed_ref, 1, 2 * pair))
        for side in range(2):
            row = 2 * pair + side
            send_ref[0, row] = (halves(y2[0])[side] + halves(y3[1])[side]).astype(BF16)
            send_ref[1, row] = halves(y3[0])[side].astype(BF16)
            base_ref[0, row] = halves(y2[2])[side] + bias + stream_ref[2, row].astype(F32)
            base_ref[1, row] = (
                halves(y2[1])[side] + halves(y3[2])[side] + bias + stream_ref[3, row].astype(F32)
            )


def history_kernel(
    earlier_ref, above_ref, below_ref, hidden_ref, base_ref, stream_ref, weights_ref, gain_ref, bias_ref,
    out_ref, first_ref,
    taps_ref, normed_ref,
):
    rows = earlier_ref.shape[1]
    band = lax.axis_index("rows")
    keep_above = jnp.where(band > 0, 1.0, 0.0)
    keep_below = jnp.where(band < lax.axis_size("rows") - 1, 1.0, 0.0)
    gain = gain_ref[0]
    for frame in range(2):
        for row in range(rows + 4):
            if row < 2:
                values = above_ref[frame, row]
            elif row < rows + 2:
                values = earlier_ref[frame, row - 2]
            else:
                values = below_ref[frame, row - rows - 2]
            store_taps(taps_ref, frame, row, activated(values.astype(F32), gain))
    gain = gain_ref[1]
    for pair in range((rows + 2) // 2):
        y0 = tap_products(weights_ref, 0, (0, 0), row_pair(taps_ref, 0, 2 * pair))
        y1 = tap_products(weights_ref, 0, (0, 1), row_pair(taps_ref, 1, 2 * pair))
        hidden = [y0[0] + y1[1], y1[0]]
        for frame in range(2):
            for side, values in enumerate(halves(hidden[frame])):
                row = 2 * pair + side
                act = activated(values + hidden_ref[frame, row], gain)
                if row == 0:
                    act = act * keep_above
                if row == rows + 1:
                    act = act * keep_below
                store_taps(normed_ref, frame, row, act)
    bias = bias_ref[1]
    for pair in range(rows // 2):
        y0 = tap_products(weights_ref, 1, (0, 2), row_pair(normed_ref, 0, 2 * pair))
        y1 = tap_products(weights_ref, 1, (0, 2), row_pair(normed_ref, 1, 2 * pair))
        for side in range(2):
            row = 2 * pair + side
            first_ref[0, row] = halves(y0[2])[side] + bias + stream_ref[0, row].astype(F32)
            first_ref[1, row] = (
                halves(y0[1])[side] + halves(y1[2])[side] + bias + stream_ref[1, row].astype(F32)
            )
            out_ref[2, row] = (
                base_ref[0, row] + halves(y0[0])[side] + halves(y1[1])[side]
            ).astype(BF16)
            out_ref[3, row] = (base_ref[1, row] + halves(y1[0])[side]).astype(BF16)


def finish_kernel(partial_ref, first_ref, _, out_ref):
    out_ref[...] = (first_ref[...] + partial_ref[...].astype(F32)).astype(BF16)


def call(kernel, outs, scratch=(), flops=0, moved=0):
    return pl.pallas_call(
        kernel,
        out_shape=[jax.ShapeDtypeStruct(*out) for out in outs],
        scratch_shapes=list(scratch),
        compiler_params=pltpu.CompilerParams(vmem_limit_bytes=VMEM_BYTES),
        cost_estimate=pl.CostEstimate(flops=flops, bytes_accessed=moved, transcendentals=0),
    )


def steps(axis, distance):
    size = lax.axis_size(axis)
    return [(i, i + distance) for i in range(size) if 0 <= i + distance < size]


def row_edges(block):
    rows = block.shape[1]
    above = lax.ppermute(block[:, rows - 2 :], "rows", steps("rows", 1))
    below = lax.ppermute(block[:, :2], "rows", steps("rows", -1))
    return above, below


def shards(stream, gains, kernels, biases):
    frames, rows, channels, cols = stream.shape
    plane = (channels, cols)
    cells = rows * cols
    mac = 2 * 9 * channels * channels
    earlier = lax.ppermute(stream[frames - 2 :], "tm", steps("tm", 1))
    above, below = row_edges(stream)
    weights, gain, bias = call(
        prepare_kernel,
        [
            ((2, 3 * channels, 9 * channels), BF16),
            ((2, *plane), F32),
            ((2, *plane), F32),
        ],
        flops=10**6,
        moved=0,
    )(kernels.reshape(2, 3, 9 * channels, channels), gains, biases)
    sent, hidden, base = call(
        local_kernel,
        [
            ((2, rows, *plane), BF16),
            ((2, rows + 2, *plane), F32),
            ((2, rows, *plane), F32),
        ],
        [
            pltpu.VMEM((frames, rows + 4, 3 * channels, cols), BF16),
            pltpu.VMEM((2, rows + 2, 3 * channels, cols), BF16),
        ],
        flops=0,
        moved=0,
    )(stream, above, below, weights, gain, bias)
    partial = lax.ppermute(sent, "tm", steps("tm", 1))
    above, below = row_edges(earlier)
    out, first = call(
        history_kernel,
        [((frames, rows, *plane), BF16), ((2, rows, *plane), F32)],
        [
            pltpu.VMEM((2, rows + 4, 3 * channels, cols), BF16),
            pltpu.VMEM((2, rows + 2, 3 * channels, cols), BF16),
        ],
        flops=0,
        moved=0,
    )(earlier, above, below, hidden, base, stream, weights, gain, bias)
    block = pl.BlockSpec((2, rows, *plane), lambda i: (0, 0, 0, 0))
    return pl.pallas_call(
        finish_kernel,
        grid=(1,),
        out_shape=jax.ShapeDtypeStruct(stream.shape, BF16),
        in_specs=[block, block, pl.BlockSpec(memory_space=pl.ANY)],
        out_specs=block,
        input_output_aliases={2: 0},
        compiler_params=pltpu.CompilerParams(vmem_limit_bytes=VMEM_BYTES),
        cost_estimate=pl.CostEstimate(flops=10**6, bytes_accessed=2 * 10**6, transcendentals=0),
    )(partial, first, out)


def solution(mesh):
    placed = (P("tm", "rows", None, None), P(), P(), P())
    return jax.shard_map(
        shards, mesh=mesh, in_specs=placed, out_specs=P("tm", "rows", None, None), check_vma=False
    )
```

```python
import functools

import jax
import jax.numpy as jnp
from jax import lax
from jax.experimental import pallas as pl
from jax.experimental.pallas import tpu as pltpu
from jax.sharding import PartitionSpec as P

EPS = 1e-06
VMEM_BYTES = 20 * 1024 * 1024
F32 = jnp.float32
BF16 = jnp.bfloat16


def activated(values, gain):
    mean_sq = jnp.mean(values * values, axis=0, keepdims=True)
    half = values * lax.rsqrt(mean_sq + EPS) * (0.5 * gain)
    return half + half * jnp.tanh(half)


def store_taps(ref, frame, row, act):
    channels, cols = act.shape
    lane = lax.broadcasted_iota(jnp.int32, act.shape, 1)
    left = jnp.where(lane == 0, 0.0, pltpu.roll(act, 1, 1))
    right = jnp.where(lane == cols - 1, 0.0, pltpu.roll(act, cols - 1, 1))
    ref[frame, row, 0:channels] = left.astype(BF16)
    ref[frame, row, channels : 2 * channels] = act.astype(BF16)
    ref[frame, row, 2 * channels :] = right.astype(BF16)


def row_pair(ref, frame, row):
    depth, cols = ref.shape[2], ref.shape[3]
    first = ref[frame, row : row + 3].reshape(3 * depth, cols)
    second = ref[frame, row + 1 : row + 4].reshape(3 * depth, cols)
    return jnp.concatenate([first, second], axis=1)


def tap_products(weights_ref, index, taps, columns):
    channels = weights_ref.shape[1] // 3
    low, high = taps
    product = jnp.dot(
        weights_ref[index, low * channels : (high + 1) * channels],
        columns,
        preferred_element_type=F32,
    )
    return {
        tap: product[(tap - low) * channels : (tap - low + 1) * channels]
        for tap in range(low, high + 1)
    }


def prepare_kernel(kernels_ref, gains_ref, biases_ref, weights_ref, gain_ref, bias_ref):
    channels = gains_ref.shape[1]
    cols = gain_ref.shape[2]
    for index in range(2):
        for tap in range(3):
            weights_ref[index, tap * channels : (tap + 1) * channels, :] = kernels_ref[index, tap].T
        for source, target in ((gains_ref, gain_ref), (biases_ref, bias_ref)):
            spread = jnp.broadcast_to(source[index : index + 1], (cols, channels))
            target[index] = spread.T


def halves(pair):
    cols = pair.shape[1] // 2
    return pair[:, :cols], pair[:, cols:]


def activate_rows(taps_ref, frames, odd, own, partner_ref, across, gain):
    rows = taps_ref.shape[1] - 4
    for frame in range(frames):
        for row in range(rows + 4):
            if row < 2:
                values = jnp.where(odd, partner_ref[frame, row], across(frame, row, 0))
            elif row < rows + 2:
                values = own(frame, row - 2)
            else:
                edge = row - rows - 2
                values = jnp.where(odd, across(frame, edge, rows), partner_ref[frame, edge])
            store_taps(taps_ref, frame, row, activated(values.astype(F32), gain))


def widen_kernel(stream_ref, across_ref, out_ref):
    frames, rows = stream_ref.shape[:2]
    odd = lax.axis_index("rows") % 2 == 1
    for frame in range(2):
        source = frames - 2 + frame
        out_ref[frame, pl.ds(jnp.where(odd, 0, 2), rows)] = stream_ref[source]
        out_ref[frame, pl.ds(jnp.where(odd, rows, 0), 2)] = across_ref[source]


def halo_source():
    band = lax.axis_index("rows")
    outer_band = (band == 0) | (band == lax.axis_size("rows") - 1)
    first_block = lax.axis_index("tm") % span("tm") == 0
    return outer_band, outer_band & first_block


def edge_kernel(outer_ref, relayed_ref, inner_ref, out_ref):
    rows = outer_ref.shape[1]
    outer_band, relay = halo_source()
    odd = lax.axis_index("rows") % 2 == 1
    near = pl.ds(jnp.where(odd, 0, rows - 2), 2)
    wide = pl.ds(jnp.where(odd, 0, rows), 2)
    direct = jnp.where(outer_band, outer_ref[:, near], inner_ref[:, wide])
    out_ref[...] = jnp.where(relay, relayed_ref[:, near], direct)


def local_kernel(
    stream_ref, partner_ref, across_ref, weights_ref, gain_ref, bias_ref,
    send_ref, hidden_ref, base_ref,
    taps_ref, normed_ref,
):
    frames, rows = stream_ref.shape[:2]
    band = lax.axis_index("rows")
    keep_above = jnp.where(band > 0, 1.0, 0.0)
    keep_below = jnp.where(band < lax.axis_size("rows") - 1, 1.0, 0.0)
    odd = band % 2 == 1
    gain = gain_ref[0]

    activate_rows(
        taps_ref,
        frames,
        odd,
        lambda frame, row: stream_ref[frame, row],
        partner_ref,
        lambda frame, row, _: across_ref[frame, row],
        gain,
    )
    gain = gain_ref[1]
    bias = jnp.concatenate([bias_ref[0]] * 2, axis=1)
    for pair in range((rows + 2) // 2):
        y = [
            tap_products(weights_ref, 0, taps, row_pair(taps_ref, frame, 2 * pair))
            for frame, taps in enumerate(((0, 2), (0, 2), (1, 2), (2, 2)))
        ]
        hidden = [
            y[0][2] + bias,
            y[0][1] + y[1][2] + bias,
            y[0][0] + y[1][1] + y[2][2] + bias,
            y[1][0] + y[2][1] + y[3][2] + bias,
        ]
        for frame in range(4):
            for side, values in enumerate(halves(hidden[frame])):
                row = 2 * pair + side
                if frame < 2:
                    hidden_ref[frame, row] = values
                    continue
                act = activated(values, gain)
                if row == 0:
                    act = act * keep_above
                if row == rows + 1:
                    act = act * keep_below
                store_taps(normed_ref, frame - 2, row, act)
    bias = bias_ref[1]
    for pair in range(rows // 2):
        y2 = tap_products(weights_ref, 1, (0, 2), row_pair(normed_ref, 0, 2 * pair))
        y3 = tap_products(weights_ref, 1, (0, 2), row_pair(normed_ref, 1, 2 * pair))
        for side in range(2):
            row = 2 * pair + side
            send_ref[0, row] = (halves(y2[0])[side] + halves(y3[1])[side]).astype(BF16)
            send_ref[1, row] = halves(y3[0])[side].astype(BF16)
            base_ref[0, row] = halves(y2[2])[side] + bias + stream_ref[2, row].astype(F32)
            base_ref[1, row] = (
                halves(y2[1])[side] + halves(y3[2])[side] + bias + stream_ref[3, row].astype(F32)
            )


def history_kernel(
    outer_ref, relayed_ref, inner_ref, partner_ref, hidden_ref, base_ref, stream_ref, weights_ref, gain_ref, bias_ref,
    out_ref, first_ref,
    taps_ref, normed_ref,
):
    rows = outer_ref.shape[1]
    band = lax.axis_index("rows")
    keep_above = jnp.where(band > 0, 1.0, 0.0)
    keep_below = jnp.where(band < lax.axis_size("rows") - 1, 1.0, 0.0)
    odd = band % 2 == 1
    gain = gain_ref[0]

    outer_band, relay = halo_source()
    shift = jnp.where(odd, 0, 2)

    def own(frame, row):
        direct = jnp.where(outer_band, outer_ref[frame, row], inner_ref[frame, row + shift])
        return jnp.where(relay, relayed_ref[frame, row], direct)

    activate_rows(
        taps_ref,
        2,
        odd,
        own,
        partner_ref,
        lambda frame, row, start: inner_ref[frame, row + start],
        gain,
    )
    gain = gain_ref[1]
    for pair in range((rows + 2) // 2):
        y0 = tap_products(weights_ref, 0, (0, 0), row_pair(taps_ref, 0, 2 * pair))
        y1 = tap_products(weights_ref, 0, (0, 1), row_pair(taps_ref, 1, 2 * pair))
        hidden = [y0[0] + y1[1], y1[0]]
        for frame in range(2):
            for side, values in enumerate(halves(hidden[frame])):
                row = 2 * pair + side
                act = activated(values + hidden_ref[frame, row], gain)
                if row == 0:
                    act = act * keep_above
                if row == rows + 1:
                    act = act * keep_below
                store_taps(normed_ref, frame, row, act)
    bias = bias_ref[1]
    for pair in range(rows // 2):
        y0 = tap_products(weights_ref, 1, (0, 2), row_pair(normed_ref, 0, 2 * pair))
        y1 = tap_products(weights_ref, 1, (0, 2), row_pair(normed_ref, 1, 2 * pair))
        for side in range(2):
            row = 2 * pair + side
            first_ref[0, row] = halves(y0[2])[side] + bias + stream_ref[0, row].astype(F32)
            first_ref[1, row] = (
                halves(y0[1])[side] + halves(y1[2])[side] + bias + stream_ref[1, row].astype(F32)
            )
            out_ref[2, row] = (
                base_ref[0, row] + halves(y0[0])[side] + halves(y1[1])[side]
            ).astype(BF16)
            out_ref[3, row] = (base_ref[1, row] + halves(y1[0])[side]).astype(BF16)


def finish_kernel(partial_ref, first_ref, _, out_ref):
    out_ref[...] = (first_ref[...] + partial_ref[...].astype(F32)).astype(BF16)


def call(kernel, outs, scratch=(), flops=0, moved=0):
    return pl.pallas_call(
        kernel,
        out_shape=[jax.ShapeDtypeStruct(*out) for out in outs],
        scratch_shapes=list(scratch),
        compiler_params=pltpu.CompilerParams(vmem_limit_bytes=VMEM_BYTES),
        cost_estimate=pl.CostEstimate(flops=flops, bytes_accessed=moved, transcendentals=0),
    )


def span(axis):
    return lax.axis_size(axis) // 4


def steps(axis, distance):
    size = lax.axis_size(axis)
    return [(i, i + distance) for i in range(size) if 0 <= i + distance < size]


def spread(pairs, bands):
    size = lax.axis_size("rows")
    return [(i * size + source, j * size + target) for i, j in pairs for source, target in bands]


def band_part(block, late):
    start = jnp.where(late, block.shape[1] - 2, 0)
    return lax.dynamic_slice_in_dim(block, start, 2, axis=1)


def partners(block):
    return lax.ppermute(block, "rows", [(0, 1), (1, 0), (2, 3), (3, 2)])


def shards(stream, gains, kernels, biases):
    frames, rows, channels, cols = stream.shape
    plane = (channels, cols)
    cells = rows * cols
    mac = 2 * 9 * channels * channels
    odd = lax.axis_index("rows") % 2 == 1
    following = steps("tm", 1)
    across = lax.ppermute(band_part(stream, odd), "rows", [(1, 2), (2, 1)])
    mesh_axes = ("tm", "rows")
    outer_bands, inner_bands = [(0, 0), (3, 3)], [(1, 1), (2, 2)]
    size, group = lax.axis_size("tm"), span("tm")
    detour = [(i, i + 1 if (i + 1) % group else i + 1 - group) for i in range(size - 1)]
    onward = [(i, i + group) for i in range(0, size - group, group)]
    outer = lax.ppermute(stream[frames - 2 :], mesh_axes, spread(detour, outer_bands))
    partner = partners(band_part(stream, ~odd))
    (widened,) = call(widen_kernel, [((2, rows + 2, *plane), BF16)])(stream, across)
    inner = lax.ppermute(widened, mesh_axes, spread(following, inner_bands))
    weights, gain, bias = call(
        prepare_kernel,
        [
            ((2, 3 * channels, 9 * channels), BF16),
            ((2, *plane), F32),
            ((2, *plane), F32),
        ],
        flops=10**6,
        moved=0,
    )(kernels.reshape(2, 3, 9 * channels, channels), gains, biases)
    sent, hidden, base = call(
        local_kernel,
        [
            ((2, rows, *plane), BF16),
            ((2, rows + 2, *plane), F32),
            ((2, rows, *plane), F32),
        ],
        [
            pltpu.VMEM((frames, rows + 4, 3 * channels, cols), BF16),
            pltpu.VMEM((2, rows + 2, 3 * channels, cols), BF16),
        ],
        flops=0,
        moved=0,
    )(stream, partner, across, weights, gain, bias)
    sent, outer = lax.optimization_barrier((sent, outer))
    partial = lax.ppermute(sent, "tm", following)
    relayed = lax.ppermute(outer, mesh_axes, spread(onward, outer_bands))
    (edge,) = call(edge_kernel, [((2, 2, *plane), BF16)])(outer, relayed, inner)
    beside = partners(edge)
    out, first = call(
        history_kernel,
        [((frames, rows, *plane), BF16), ((2, rows, *plane), F32)],
        [
            pltpu.VMEM((2, rows + 4, 3 * channels, cols), BF16),
            pltpu.VMEM((2, rows + 2, 3 * channels, cols), BF16),
        ],
        flops=0,
        moved=0,
    )(outer, relayed, inner, beside, hidden, base, stream, weights, gain, bias)
    block = pl.BlockSpec((2, rows, *plane), lambda i: (0, 0, 0, 0))
    return pl.pallas_call(
        finish_kernel,
        grid=(1,),
        out_shape=jax.ShapeDtypeStruct(stream.shape, BF16),
        in_specs=[block, block, pl.BlockSpec(memory_space=pl.ANY)],
        out_specs=block,
        input_output_aliases={2: 0},
        compiler_params=pltpu.CompilerParams(vmem_limit_bytes=VMEM_BYTES),
        cost_estimate=pl.CostEstimate(flops=10**6, bytes_accessed=2 * 10**6, transcendentals=0),
    )(partial, first, out)


def solution(mesh):
    placed = (P("tm", "rows", None, None), P(), P(), P())
    return jax.shard_map(
        shards, mesh=mesh, in_specs=placed, out_specs=P("tm", "rows", None, None), check_vma=False
    )
```

```python
import functools

import jax
import jax.numpy as jnp
from jax import lax
from jax.experimental import pallas as pl
from jax.experimental.pallas import tpu as pltpu
from jax.sharding import PartitionSpec as P

EPS = 1e-06
VMEM_BYTES = 20 * 1024 * 1024
F32 = jnp.float32
BF16 = jnp.bfloat16


def activated(values, gain):
    mean_sq = jnp.mean(values * values, axis=0, keepdims=True)
    half = values * lax.rsqrt(mean_sq + EPS) * (0.5 * gain)
    return half + half * jnp.tanh(half)


def store_taps(ref, frame, row, act):
    channels, cols = act.shape
    lane = lax.broadcasted_iota(jnp.int32, act.shape, 1)
    left = jnp.where(lane == 0, 0.0, pltpu.roll(act, 1, 1))
    right = jnp.where(lane == cols - 1, 0.0, pltpu.roll(act, cols - 1, 1))
    ref[frame, row, 0:channels] = left.astype(BF16)
    ref[frame, row, channels : 2 * channels] = act.astype(BF16)
    ref[frame, row, 2 * channels :] = right.astype(BF16)


def row_pair(ref, frame, row):
    depth, cols = ref.shape[2], ref.shape[3]
    first = ref[frame, row : row + 3].reshape(3 * depth, cols)
    second = ref[frame, row + 1 : row + 4].reshape(3 * depth, cols)
    return jnp.concatenate([first, second], axis=1)


def tap_products(weights_ref, index, taps, columns):
    channels = weights_ref.shape[1] // 3
    low, high = taps
    product = jnp.dot(
        weights_ref[index, low * channels : (high + 1) * channels],
        columns,
        preferred_element_type=F32,
    )
    return {
        tap: product[(tap - low) * channels : (tap - low + 1) * channels]
        for tap in range(low, high + 1)
    }


def prepare_kernel(kernels_ref, gains_ref, biases_ref, weights_ref, gain_ref, bias_ref):
    channels = gains_ref.shape[1]
    cols = gain_ref.shape[2]
    for index in range(2):
        for tap in range(3):
            weights_ref[index, tap * channels : (tap + 1) * channels, :] = kernels_ref[index, tap].T
        for source, target in ((gains_ref, gain_ref), (biases_ref, bias_ref)):
            spread = jnp.broadcast_to(source[index : index + 1], (cols, channels))
            target[index] = spread.T


def halves(pair):
    cols = pair.shape[1] // 2
    return pair[:, :cols], pair[:, cols:]


def activate_rows(taps_ref, frames, odd, own, partner_ref, across, gain):
    rows = taps_ref.shape[1] - 4
    for frame in range(frames):
        for row in range(rows + 4):
            if row < 2:
                values = jnp.where(odd, partner_ref[frame, row], across(frame, row, 0))
            elif row < rows + 2:
                values = own(frame, row - 2)
            else:
                edge = row - rows - 2
                values = jnp.where(odd, across(frame, edge, rows), partner_ref[frame, edge])
            store_taps(taps_ref, frame, row, activated(values.astype(F32), gain))


def first_block_bands():
    band = lax.axis_index("rows")
    outer_band = (band == 0) | (band == lax.axis_size("rows") - 1)
    first_block = lax.axis_index("tm") % span("tm") == 0
    return first_block & outer_band, first_block & jnp.logical_not(outer_band)


def narrow_kernel(earlier_ref, out_ref):
    half = out_ref.shape[1]
    start = jnp.where(lax.axis_index("rows") == 1, half, 0)
    out_ref[...] = earlier_ref[:, pl.ds(start, half)]


def edge_kernel(earlier_ref, narrow_ref, rest_ref, out_ref):
    relay, _ = first_block_bands()
    rows = earlier_ref.shape[1]
    odd = lax.axis_index("rows") % 2 == 1
    near = pl.ds(jnp.where(odd, 0, rows - 2), 2)
    relayed = jnp.where(odd, narrow_ref[:, :2], rest_ref[:, rows // 2 - 2 :])
    out_ref[...] = jnp.where(relay, relayed, earlier_ref[:, near])


def local_kernel(
    stream_ref, partner_ref, across_ref, weights_ref, gain_ref, bias_ref,
    send_ref, hidden_ref, base_ref,
    taps_ref, normed_ref,
):
    frames, rows = stream_ref.shape[:2]
    band = lax.axis_index("rows")
    keep_above = jnp.where(band > 0, 1.0, 0.0)
    keep_below = jnp.where(band < lax.axis_size("rows") - 1, 1.0, 0.0)
    odd = band % 2 == 1
    gain = gain_ref[0]

    activate_rows(
        taps_ref,
        frames,
        odd,
        lambda frame, row: stream_ref[frame, row],
        partner_ref,
        lambda frame, row, _: across_ref[frame, row],
        gain,
    )
    gain = gain_ref[1]
    bias = jnp.concatenate([bias_ref[0]] * 2, axis=1)
    for pair in range((rows + 2) // 2):
        y = [
            tap_products(weights_ref, 0, taps, row_pair(taps_ref, frame, 2 * pair))
            for frame, taps in enumerate(((0, 2), (0, 2), (1, 2), (2, 2)))
        ]
        hidden = [
            y[0][2] + bias,
            y[0][1] + y[1][2] + bias,
            y[0][0] + y[1][1] + y[2][2] + bias,
            y[1][0] + y[2][1] + y[3][2] + bias,
        ]
        for frame in range(4):
            for side, values in enumerate(halves(hidden[frame])):
                row = 2 * pair + side
                if frame < 2:
                    hidden_ref[frame, row] = values
                    continue
                act = activated(values, gain)
                if row == 0:
                    act = act * keep_above
                if row == rows + 1:
                    act = act * keep_below
                store_taps(normed_ref, frame - 2, row, act)
    bias = bias_ref[1]
    for pair in range(rows // 2):
        y2 = tap_products(weights_ref, 1, (0, 2), row_pair(normed_ref, 0, 2 * pair))
        y3 = tap_products(weights_ref, 1, (0, 2), row_pair(normed_ref, 1, 2 * pair))
        for side in range(2):
            row = 2 * pair + side
            send_ref[0, row] = (halves(y2[0])[side] + halves(y3[1])[side]).astype(BF16)
            send_ref[1, row] = halves(y3[0])[side].astype(BF16)
            base_ref[0, row] = halves(y2[2])[side] + bias + stream_ref[2, row].astype(F32)
            base_ref[1, row] = (
                halves(y2[1])[side] + halves(y3[2])[side] + bias + stream_ref[3, row].astype(F32)
            )


def history_kernel(
    earlier_ref, narrow_ref, rest_ref, corner_ref, partner_ref, hidden_ref, base_ref, stream_ref, weights_ref, gain_ref, bias_ref,
    out_ref, first_ref,
    taps_ref, normed_ref,
):
    rows = earlier_ref.shape[1]
    band = lax.axis_index("rows")
    keep_above = jnp.where(band > 0, 1.0, 0.0)
    keep_below = jnp.where(band < lax.axis_size("rows") - 1, 1.0, 0.0)
    odd = band % 2 == 1
    gain = gain_ref[0]

    relay, swap = first_block_bands()

    def own(frame, row):
        half = rows // 2
        relayed = narrow_ref[frame, row] if row < half else rest_ref[frame, row - half]
        return jnp.where(relay, relayed, earlier_ref[frame, row])

    def across(frame, row, start):
        swapped = narrow_ref[frame, row + (rows // 2 - 2 if start == 0 else 0)]
        return jnp.where(swap, swapped, corner_ref[frame, row])

    activate_rows(
        taps_ref,
        2,
        odd,
        own,
        partner_ref,
        across,
        gain,
    )
    gain = gain_ref[1]
    for pair in range((rows + 2) // 2):
        y0 = tap_products(weights_ref, 0, (0, 0), row_pair(taps_ref, 0, 2 * pair))
        y1 = tap_products(weights_ref, 0, (0, 1), row_pair(taps_ref, 1, 2 * pair))
        hidden = [y0[0] + y1[1], y1[0]]
        for frame in range(2):
            for side, values in enumerate(halves(hidden[frame])):
                row = 2 * pair + side
                act = activated(values + hidden_ref[frame, row], gain)
                if row == 0:
                    act = act * keep_above
                if row == rows + 1:
                    act = act * keep_below
                store_taps(normed_ref, frame, row, act)
    bias = bias_ref[1]
    for pair in range(rows // 2):
        y0 = tap_products(weights_ref, 1, (0, 2), row_pair(normed_ref, 0, 2 * pair))
        y1 = tap_products(weights_ref, 1, (0, 2), row_pair(normed_ref, 1, 2 * pair))
        for side in range(2):
            row = 2 * pair + side
            first_ref[0, row] = halves(y0[2])[side] + bias + stream_ref[0, row].astype(F32)
            first_ref[1, row] = (
                halves(y0[1])[side] + halves(y1[2])[side] + bias + stream_ref[1, row].astype(F32)
            )
            out_ref[2, row] = (
                base_ref[0, row] + halves(y0[0])[side] + halves(y1[1])[side]
            ).astype(BF16)
            out_ref[3, row] = (base_ref[1, row] + halves(y1[0])[side]).astype(BF16)


def finish_kernel(partial_ref, first_ref, _, out_ref):
    out_ref[...] = (first_ref[...] + partial_ref[...].astype(F32)).astype(BF16)


def call(kernel, outs, scratch=(), flops=0, moved=0):
    return pl.pallas_call(
        kernel,
        out_shape=[jax.ShapeDtypeStruct(*out) for out in outs],
        scratch_shapes=list(scratch),
        compiler_params=pltpu.CompilerParams(vmem_limit_bytes=VMEM_BYTES),
        cost_estimate=pl.CostEstimate(flops=flops, bytes_accessed=moved, transcendentals=0),
    )


def span(axis):
    return lax.axis_size(axis) // 4


def steps(axis, distance):
    size = lax.axis_size(axis)
    return [(i, i + distance) for i in range(size) if 0 <= i + distance < size]


def spread(pairs, bands):
    size = lax.axis_size("rows")
    return [(i * size + source, j * size + target) for i, j in pairs for source, target in bands]


def band_part(block, late):
    start = jnp.where(late, block.shape[1] - 2, 0)
    return lax.dynamic_slice_in_dim(block, start, 2, axis=1)


def partners(block):
    return lax.ppermute(block, "rows", [(0, 1), (1, 0), (2, 3), (3, 2)])


def shards(stream, gains, kernels, biases):
    frames, rows, channels, cols = stream.shape
    plane = (channels, cols)
    cells = rows * cols
    mac = 2 * 9 * channels * channels
    odd = lax.axis_index("rows") % 2 == 1
    following = steps("tm", 1)
    across = lax.ppermute(band_part(stream, odd), "rows", [(1, 2), (2, 1)])
    mesh_axes = ("tm", "rows")
    outer_bands, inner_bands = [(0, 0), (3, 3)], [(1, 1), (2, 2)]
    size, group = lax.axis_size("tm"), span("tm")
    onward = [(i, i + group) for i in range(0, size - group, group)]
    crossing = [(i, j) for i, j in following if j % group == 0]
    straight = [(i, j) for i, j in following if j % group]
    turned = [(i, j - group) for i, j in crossing]
    first_blocks = [(j, j) for _, j in crossing]
    earlier = lax.ppermute(
        stream[frames - 2 :],
        mesh_axes,
        spread(straight, outer_bands + inner_bands)
        + spread(turned, outer_bands)
        + spread(crossing, inner_bands),
    )
    partner = partners(band_part(stream, ~odd))
    weights, gain, bias = call(
        prepare_kernel,
        [
            ((2, 3 * channels, 9 * channels), BF16),
            ((2, *plane), F32),
            ((2, *plane), F32),
        ],
        flops=10**6,
        moved=0,
    )(kernels.reshape(2, 3, 9 * channels, channels), gains, biases)
    sent, hidden, base = call(
        local_kernel,
        [
            ((2, rows, *plane), BF16),
            ((2, rows + 2, *plane), F32),
            ((2, rows, *plane), F32),
        ],
        [
            pltpu.VMEM((frames, rows + 4, 3 * channels, cols), BF16),
            pltpu.VMEM((2, rows + 2, 3 * channels, cols), BF16),
        ],
        flops=0,
        moved=0,
    )(stream, partner, across, weights, gain, bias)
    corner, sent = lax.optimization_barrier((across[frames - 2 :], sent))
    partial = lax.ppermute(sent, "tm", following)
    corner = lax.ppermute(corner, mesh_axes, spread(straight, inner_bands))
    earlier, corner = lax.optimization_barrier((earlier, corner))
    half = rows // 2
    (narrow,) = call(narrow_kernel, [((2, half, *plane), BF16)])(earlier)
    narrow = lax.ppermute(
        narrow, mesh_axes, spread(onward, outer_bands) + spread(first_blocks, [(1, 2), (2, 1)])
    )
    rest = lax.ppermute(earlier[:, half:], mesh_axes, spread(onward, outer_bands))
    (edge,) = call(edge_kernel, [((2, 2, *plane), BF16)])(earlier, narrow, rest)
    beside = partners(edge)
    out, first = call(
        history_kernel,
        [((frames, rows, *plane), BF16), ((2, rows, *plane), F32)],
        [
            pltpu.VMEM((2, rows + 4, 3 * channels, cols), BF16),
            pltpu.VMEM((2, rows + 2, 3 * channels, cols), BF16),
        ],
        flops=0,
        moved=0,
    )(earlier, narrow, rest, corner, beside, hidden, base, stream, weights, gain, bias)
    block = pl.BlockSpec((2, rows, *plane), lambda i: (0, 0, 0, 0))
    return pl.pallas_call(
        finish_kernel,
        grid=(1,),
        out_shape=jax.ShapeDtypeStruct(stream.shape, BF16),
        in_specs=[block, block, pl.BlockSpec(memory_space=pl.ANY)],
        out_specs=block,
        input_output_aliases={2: 0},
        compiler_params=pltpu.CompilerParams(vmem_limit_bytes=VMEM_BYTES),
        cost_estimate=pl.CostEstimate(flops=10**6, bytes_accessed=2 * 10**6, transcendentals=0),
    )(partial, first, out)


def solution(mesh):
    placed = (P("tm", "rows", None, None), P(), P(), P())
    return jax.shard_map(
        shards, mesh=mesh, in_specs=placed, out_specs=P("tm", "rows", None, None), check_vma=False
    )
```

```python
import functools

import jax
import jax.numpy as jnp
from jax import lax
from jax.experimental import pallas as pl
from jax.experimental.pallas import tpu as pltpu
from jax.sharding import PartitionSpec as P

EPS = 1e-06
VMEM_BYTES = 20 * 1024 * 1024
F32 = jnp.float32
BF16 = jnp.bfloat16


def activated(values, gain):
    mean_sq = jnp.mean(values * values, axis=0, keepdims=True)
    half = values * lax.rsqrt(mean_sq + EPS) * (0.5 * gain)
    return half + half * jnp.tanh(half)


def store_taps(ref, frame, row, act):
    channels, cols = act.shape
    lane = lax.broadcasted_iota(jnp.int32, act.shape, 1)
    left = jnp.where(lane == 0, 0.0, pltpu.roll(act, 1, 1))
    right = jnp.where(lane == cols - 1, 0.0, pltpu.roll(act, cols - 1, 1))
    ref[frame, row, 0:channels] = left.astype(BF16)
    ref[frame, row, channels : 2 * channels] = act.astype(BF16)
    ref[frame, row, 2 * channels :] = right.astype(BF16)


def row_pair(ref, frame, row):
    depth, cols = ref.shape[2], ref.shape[3]
    first = ref[frame, row : row + 3].reshape(3 * depth, cols)
    second = ref[frame, row + 1 : row + 4].reshape(3 * depth, cols)
    return jnp.concatenate([first, second], axis=1)


def tap_products(weights_ref, index, taps, columns):
    channels = weights_ref.shape[1] // 3
    low, high = taps
    product = jnp.dot(
        weights_ref[index, low * channels : (high + 1) * channels],
        columns,
        preferred_element_type=F32,
    )
    return {
        tap: product[(tap - low) * channels : (tap - low + 1) * channels]
        for tap in range(low, high + 1)
    }


def cut_kernel(stream_ref, recent_ref, across_ref, partner_ref, sems):
    frames, rows = stream_ref.shape[:2]
    odd = lax.axis_index("rows") % 2 == 1
    outward = pl.ds(jnp.where(odd, rows - 2, 0), 2)
    inward = pl.ds(jnp.where(odd, 0, rows - 2), 2)
    copies = [
        pltpu.make_async_copy(stream_ref.at[pl.ds(frames - 2, 2)], recent_ref, sems.at[0]),
        pltpu.make_async_copy(stream_ref.at[:, outward], across_ref, sems.at[1]),
        pltpu.make_async_copy(stream_ref.at[:, inward], partner_ref, sems.at[2]),
    ]
    for copy in copies:
        copy.start()
    for copy in copies:
        copy.wait()


def prepare_kernel(
    all_kernels_ref, all_gains_ref, all_biases_ref,
    weights_ref, gain_ref, bias_ref,
    kernels_ref, gains_ref, biases_ref, sems,
):
    copies = [
        pltpu.make_async_copy(all_kernels_ref, kernels_ref, sems.at[0]),
        pltpu.make_async_copy(all_gains_ref, gains_ref, sems.at[1]),
        pltpu.make_async_copy(all_biases_ref, biases_ref, sems.at[2]),
    ]
    for copy in copies:
        copy.start()
    for copy in copies:
        copy.wait()
    channels = gains_ref.shape[1]
    cols = gain_ref.shape[2]
    for index in range(2):
        for tap in range(3):
            weights_ref[index, tap * channels : (tap + 1) * channels, :] = kernels_ref[index, tap].T
        for source, target in ((gains_ref, gain_ref), (biases_ref, bias_ref)):
            spread = jnp.broadcast_to(source[index : index + 1], (cols, channels))
            target[index] = spread.T


def halves(pair):
    cols = pair.shape[1] // 2
    return pair[:, :cols], pair[:, cols:]


def activate_rows(taps_ref, frames, odd, own, partner_ref, across, gain):
    rows = taps_ref.shape[1] - 4
    for frame in range(frames):
        for row in range(rows + 4):
            if row < 2:
                values = jnp.where(odd, partner_ref[frame, row], across(frame, row, 0))
            elif row < rows + 2:
                values = own(frame, row - 2)
            else:
                edge = row - rows - 2
                values = jnp.where(odd, across(frame, edge, rows), partner_ref[frame, edge])
            store_taps(taps_ref, frame, row, activated(values.astype(F32), gain))


def first_block_bands():
    band = lax.axis_index("rows")
    outer_band = (band == 0) | (band == lax.axis_size("rows") - 1)
    first_block = lax.axis_index("tm") % span("tm") == 0
    return first_block & outer_band, first_block & jnp.logical_not(outer_band)


def narrow_kernel(earlier_ref, out_ref):
    half = out_ref.shape[1]
    start = jnp.where(lax.axis_index("rows") == 1, half, 0)
    out_ref[...] = earlier_ref[:, pl.ds(start, half)]


def edge_kernel(earlier_ref, narrow_ref, rest_ref, out_ref):
    relay, _ = first_block_bands()
    rows = earlier_ref.shape[1]
    odd = lax.axis_index("rows") % 2 == 1
    near = pl.ds(jnp.where(odd, 0, rows - 2), 2)
    relayed = jnp.where(odd, narrow_ref[:, :2], rest_ref[:, rows // 2 - 2 :])
    out_ref[...] = jnp.where(relay, relayed, earlier_ref[:, near])


def local_kernel(
    stream_ref, partner_ref, across_ref, weights_ref, gain_ref, bias_ref,
    send_ref, hidden_ref, base_ref,
    taps_ref, normed_ref,
):
    frames, rows = stream_ref.shape[:2]
    band = lax.axis_index("rows")
    keep_above = jnp.where(band > 0, 1.0, 0.0)
    keep_below = jnp.where(band < lax.axis_size("rows") - 1, 1.0, 0.0)
    odd = band % 2 == 1
    gain = gain_ref[0]

    activate_rows(
        taps_ref,
        frames,
        odd,
        lambda frame, row: stream_ref[frame, row],
        partner_ref,
        lambda frame, row, _: across_ref[frame, row],
        gain,
    )
    gain = gain_ref[1]
    bias = jnp.concatenate([bias_ref[0]] * 2, axis=1)
    for pair in range((rows + 2) // 2):
        y = [
            tap_products(weights_ref, 0, taps, row_pair(taps_ref, frame, 2 * pair))
            for frame, taps in enumerate(((0, 2), (0, 2), (1, 2), (2, 2)))
        ]
        hidden = [
            y[0][2] + bias,
            y[0][1] + y[1][2] + bias,
            y[0][0] + y[1][1] + y[2][2] + bias,
            y[1][0] + y[2][1] + y[3][2] + bias,
        ]
        for frame in range(4):
            for side, values in enumerate(halves(hidden[frame])):
                row = 2 * pair + side
                if frame < 2:
                    hidden_ref[frame, row] = values
                    continue
                act = activated(values, gain)
                if row == 0:
                    act = act * keep_above
                if row == rows + 1:
                    act = act * keep_below
                store_taps(normed_ref, frame - 2, row, act)
    bias = bias_ref[1]
    for pair in range(rows // 2):
        y2 = tap_products(weights_ref, 1, (0, 2), row_pair(normed_ref, 0, 2 * pair))
        y3 = tap_products(weights_ref, 1, (0, 2), row_pair(normed_ref, 1, 2 * pair))
        for side in range(2):
            row = 2 * pair + side
            send_ref[0, row] = (halves(y2[0])[side] + halves(y3[1])[side]).astype(BF16)
            send_ref[1, row] = halves(y3[0])[side].astype(BF16)
            base_ref[0, row] = halves(y2[2])[side] + bias + stream_ref[2, row].astype(F32)
            base_ref[1, row] = (
                halves(y2[1])[side] + halves(y3[2])[side] + bias + stream_ref[3, row].astype(F32)
            )


def history_kernel(
    earlier_ref, narrow_ref, rest_ref, corner_ref, partner_ref, hidden_ref, base_ref, stream_ref, weights_ref, gain_ref, bias_ref,
    out_ref, first_ref,
    taps_ref, normed_ref,
):
    rows = earlier_ref.shape[1]
    band = lax.axis_index("rows")
    keep_above = jnp.where(band > 0, 1.0, 0.0)
    keep_below = jnp.where(band < lax.axis_size("rows") - 1, 1.0, 0.0)
    odd = band % 2 == 1
    gain = gain_ref[0]

    relay, swap = first_block_bands()

    def own(frame, row):
        half = rows // 2
        relayed = narrow_ref[frame, row] if row < half else rest_ref[frame, row - half]
        return jnp.where(relay, relayed, earlier_ref[frame, row])

    def across(frame, row, start):
        swapped = narrow_ref[frame, row + (rows // 2 - 2 if start == 0 else 0)]
        return jnp.where(swap, swapped, corner_ref[frame, row])

    activate_rows(
        taps_ref,
        2,
        odd,
        own,
        partner_ref,
        across,
        gain,
    )
    gain = gain_ref[1]
    for pair in range((rows + 2) // 2):
        y0 = tap_products(weights_ref, 0, (0, 0), row_pair(taps_ref, 0, 2 * pair))
        y1 = tap_products(weights_ref, 0, (0, 1), row_pair(taps_ref, 1, 2 * pair))
        hidden = [y0[0] + y1[1], y1[0]]
        for frame in range(2):
            for side, values in enumerate(halves(hidden[frame])):
                row = 2 * pair + side
                act = activated(values + hidden_ref[frame, row], gain)
                if row == 0:
                    act = act * keep_above
                if row == rows + 1:
                    act = act * keep_below
                store_taps(normed_ref, frame, row, act)
    bias = bias_ref[1]
    for pair in range(rows // 2):
        y0 = tap_products(weights_ref, 1, (0, 2), row_pair(normed_ref, 0, 2 * pair))
        y1 = tap_products(weights_ref, 1, (0, 2), row_pair(normed_ref, 1, 2 * pair))
        for side in range(2):
            row = 2 * pair + side
            first_ref[0, row] = halves(y0[2])[side] + bias + stream_ref[0, row].astype(F32)
            first_ref[1, row] = (
                halves(y0[1])[side] + halves(y1[2])[side] + bias + stream_ref[1, row].astype(F32)
            )
            out_ref[2, row] = (
                base_ref[0, row] + halves(y0[0])[side] + halves(y1[1])[side]
            ).astype(BF16)
            out_ref[3, row] = (base_ref[1, row] + halves(y1[0])[side]).astype(BF16)


def finish_kernel(partial_ref, first_ref, _, out_ref):
    out_ref[...] = (first_ref[...] + partial_ref[...].astype(F32)).astype(BF16)


def call(kernel, outs, scratch=(), flops=0, moved=0):
    return pl.pallas_call(
        kernel,
        out_shape=[jax.ShapeDtypeStruct(*out) for out in outs],
        scratch_shapes=list(scratch),
        compiler_params=pltpu.CompilerParams(vmem_limit_bytes=VMEM_BYTES),
        cost_estimate=pl.CostEstimate(flops=flops, bytes_accessed=moved, transcendentals=0),
    )


def span(axis):
    return lax.axis_size(axis) // 4


def steps(axis, distance):
    size = lax.axis_size(axis)
    return [(i, i + distance) for i in range(size) if 0 <= i + distance < size]


def spread(pairs, bands):
    size = lax.axis_size("rows")
    return [(i * size + source, j * size + target) for i, j in pairs for source, target in bands]


def partners(block):
    return lax.ppermute(block, "rows", [(0, 1), (1, 0), (2, 3), (3, 2)])


def shards(stream, gains, kernels, biases):
    frames, rows, channels, cols = stream.shape
    plane = (channels, cols)
    cells = rows * cols
    mac = 2 * 9 * channels * channels
    edges = jax.ShapeDtypeStruct((frames, 2, *plane), BF16)
    recent, upper, lower = pl.pallas_call(
        cut_kernel,
        out_shape=[jax.ShapeDtypeStruct((2, rows, *plane), BF16), edges, edges],
        in_specs=[pl.BlockSpec(memory_space=pltpu.HBM)],
        scratch_shapes=[pltpu.SemaphoreType.DMA((3,))],
        compiler_params=pltpu.CompilerParams(vmem_limit_bytes=4 * 1024 * 1024),
    )(stream)
    following = steps("tm", 1)
    across = lax.ppermute(upper, "rows", [(1, 2), (2, 1)])
    mesh_axes = ("tm", "rows")
    outer_bands, inner_bands = [(0, 0), (3, 3)], [(1, 1), (2, 2)]
    size, group = lax.axis_size("tm"), span("tm")
    onward = [(i, i + group) for i in range(0, size - group, group)]
    crossing = [(i, j) for i, j in following if j % group == 0]
    straight = [(i, j) for i, j in following if j % group]
    turned = [(i, j - group) for i, j in crossing]
    first_blocks = [(j, j) for _, j in crossing]
    earlier = lax.ppermute(
        recent,
        mesh_axes,
        spread(straight, outer_bands + inner_bands)
        + spread(turned, outer_bands)
        + spread(crossing, inner_bands),
    )
    partner = partners(lower)
    taps = kernels.reshape(2, 3, 9 * channels, channels)
    weights, gain, bias = pl.pallas_call(
        prepare_kernel,
        out_shape=[
            jax.ShapeDtypeStruct((2, 3 * channels, 9 * channels), BF16),
            jax.ShapeDtypeStruct((2, *plane), F32),
            jax.ShapeDtypeStruct((2, *plane), F32),
        ],
        in_specs=[pl.BlockSpec(memory_space=pltpu.HBM)] * 3,
        scratch_shapes=[
            pltpu.VMEM(taps.shape, BF16),
            pltpu.VMEM(gains.shape, F32),
            pltpu.VMEM(biases.shape, F32),
            pltpu.SemaphoreType.DMA((3,)),
        ],
        compiler_params=pltpu.CompilerParams(vmem_limit_bytes=VMEM_BYTES),
        cost_estimate=pl.CostEstimate(flops=10**6, bytes_accessed=0, transcendentals=0),
    )(taps, gains, biases)
    sent, hidden, base = call(
        local_kernel,
        [
            ((2, rows, *plane), BF16),
            ((2, rows + 2, *plane), F32),
            ((2, rows, *plane), F32),
        ],
        [
            pltpu.VMEM((frames, rows + 4, 3 * channels, cols), BF16),
            pltpu.VMEM((2, rows + 2, 3 * channels, cols), BF16),
        ],
        flops=0,
        moved=0,
    )(stream, partner, across, weights, gain, bias)
    partial = lax.ppermute(sent, "tm", following)
    corner, sent = lax.optimization_barrier((across[frames - 2 :], sent))
    corner = lax.ppermute(corner, mesh_axes, spread(straight, inner_bands))
    earlier, sent = lax.optimization_barrier((earlier, sent))
    half = rows // 2
    (narrow,) = call(narrow_kernel, [((2, half, *plane), BF16)])(earlier)
    narrow = lax.ppermute(
        narrow, mesh_axes, spread(onward, outer_bands) + spread(first_blocks, [(1, 2), (2, 1)])
    )
    rest = lax.ppermute(earlier[:, half:], mesh_axes, spread(onward, outer_bands))
    (edge,) = call(edge_kernel, [((2, 2, *plane), BF16)])(earlier, narrow, rest)
    beside = partners(edge)
    out, first = call(
        history_kernel,
        [((frames, rows, *plane), BF16), ((2, rows, *plane), F32)],
        [
            pltpu.VMEM((2, rows + 4, 3 * channels, cols), BF16),
            pltpu.VMEM((2, rows + 2, 3 * channels, cols), BF16),
        ],
        flops=0,
        moved=0,
    )(earlier, narrow, rest, corner, beside, hidden, base, stream, weights, gain, bias)
    block = pl.BlockSpec((2, rows, *plane), lambda i: (0, 0, 0, 0))
    return pl.pallas_call(
        finish_kernel,
        grid=(1,),
        out_shape=jax.ShapeDtypeStruct(stream.shape, BF16),
        in_specs=[block, block, pl.BlockSpec(memory_space=pl.ANY)],
        out_specs=block,
        input_output_aliases={2: 0},
        compiler_params=pltpu.CompilerParams(vmem_limit_bytes=VMEM_BYTES),
        cost_estimate=pl.CostEstimate(flops=10**6, bytes_accessed=2 * 10**6, transcendentals=0),
    )(partial, first, out)


def solution(mesh):
    placed = (P("tm", "rows", None, None), P(), P(), P())
    return jax.shard_map(
        shards, mesh=mesh, in_specs=placed, out_specs=P("tm", "rows", None, None), check_vma=False
    )
```

```python
import functools

import jax
import jax.numpy as jnp
from jax import lax
from jax.experimental import pallas as pl
from jax.experimental.pallas import tpu as pltpu
from jax.sharding import PartitionSpec as P

EPS = 1e-06
VMEM_BYTES = 20 * 1024 * 1024
F32 = jnp.float32
BF16 = jnp.bfloat16


def activated(values, gain):
    mean_sq = jnp.mean(values * values, axis=0, keepdims=True)
    half = values * lax.rsqrt(mean_sq + EPS) * (0.5 * gain)
    return half + half * jnp.tanh(half)


def store_taps(ref, frame, row, act):
    channels, cols = act.shape
    lane = lax.broadcasted_iota(jnp.int32, act.shape, 1)
    left = jnp.where(lane == 0, 0.0, pltpu.roll(act, 1, 1))
    right = jnp.where(lane == cols - 1, 0.0, pltpu.roll(act, cols - 1, 1))
    ref[frame, row, 0:channels] = left.astype(BF16)
    ref[frame, row, channels : 2 * channels] = act.astype(BF16)
    ref[frame, row, 2 * channels :] = right.astype(BF16)


def row_pair(ref, frame, row):
    depth, cols = ref.shape[2], ref.shape[3]
    first = ref[frame, row : row + 3].reshape(3 * depth, cols)
    second = ref[frame, row + 1 : row + 4].reshape(3 * depth, cols)
    return jnp.concatenate([first, second], axis=1)


def tap_products(weights_ref, index, taps, columns):
    channels = weights_ref.shape[1] // 3
    low, high = taps
    product = jnp.dot(
        weights_ref[index, low * channels : (high + 1) * channels],
        columns,
        preferred_element_type=F32,
    )
    return {
        tap: product[(tap - low) * channels : (tap - low + 1) * channels]
        for tap in range(low, high + 1)
    }


def cut_kernel(stream_ref, recent_ref, across_ref, partner_ref, sems):
    frames, rows = stream_ref.shape[:2]
    odd = lax.axis_index("rows") % 2 == 1
    outward = pl.ds(jnp.where(odd, rows - 2, 0), 2)
    inward = pl.ds(jnp.where(odd, 0, rows - 2), 2)
    copies = [
        pltpu.make_async_copy(stream_ref.at[pl.ds(frames - 2, 2)], recent_ref, sems.at[0]),
        pltpu.make_async_copy(stream_ref.at[:, outward], across_ref, sems.at[1]),
        pltpu.make_async_copy(stream_ref.at[:, inward], partner_ref, sems.at[2]),
    ]
    for copy in copies:
        copy.start()
    for copy in copies:
        copy.wait()


def prepare_kernel(
    all_kernels_ref, all_gains_ref, all_biases_ref,
    weights_ref, gain_ref, bias_ref,
    kernels_ref, gains_ref, biases_ref, sems,
):
    copies = [
        pltpu.make_async_copy(all_kernels_ref, kernels_ref, sems.at[0]),
        pltpu.make_async_copy(all_gains_ref, gains_ref, sems.at[1]),
        pltpu.make_async_copy(all_biases_ref, biases_ref, sems.at[2]),
    ]
    for copy in copies:
        copy.start()
    for copy in copies:
        copy.wait()
    channels = gains_ref.shape[1]
    cols = gain_ref.shape[2]
    for index in range(2):
        for tap in range(3):
            weights_ref[index, tap * channels : (tap + 1) * channels, :] = kernels_ref[index, tap].T
        for source, target in ((gains_ref, gain_ref), (biases_ref, bias_ref)):
            spread = jnp.broadcast_to(source[index : index + 1], (cols, channels))
            target[index] = spread.T


def halves(pair):
    cols = pair.shape[1] // 2
    return pair[:, :cols], pair[:, cols:]


def activate_rows(taps_ref, frames, odd, own, partner_ref, across, gain):
    rows = taps_ref.shape[1] - 4
    for frame in range(frames):
        for row in range(rows + 4):
            if row < 2:
                values = jnp.where(odd, partner_ref[frame, row], across(frame, row, 0))
            elif row < rows + 2:
                values = own(frame, row - 2)
            else:
                edge = row - rows - 2
                values = jnp.where(odd, across(frame, edge, rows), partner_ref[frame, edge])
            store_taps(taps_ref, frame, row, activated(values.astype(F32), gain))


def first_block_bands():
    band = lax.axis_index("rows")
    outer_band = (band == 0) | (band == lax.axis_size("rows") - 1)
    first_block = lax.axis_index("tm") % span("tm") == 0
    return first_block & outer_band, first_block & jnp.logical_not(outer_band)


def narrow_kernel(earlier_ref, out_ref):
    half = out_ref.shape[1]
    start = jnp.where(lax.axis_index("rows") == 1, earlier_ref.shape[1] - half, 0)
    out_ref[...] = earlier_ref[:, pl.ds(start, half)]


def edge_kernel(earlier_ref, narrow_ref, rest_ref, out_ref):
    relay, _ = first_block_bands()
    rows = earlier_ref.shape[1]
    odd = lax.axis_index("rows") % 2 == 1
    near = pl.ds(jnp.where(odd, 0, rows - 2), 2)
    relayed = jnp.where(odd, narrow_ref[:, :2], rest_ref[:, rest_ref.shape[1] - 2 :])
    out_ref[...] = jnp.where(relay, relayed, earlier_ref[:, near])


def local_kernel(
    stream_ref, partner_ref, across_ref, weights_ref, gain_ref, bias_ref,
    send_ref, hidden_ref, base_ref,
    taps_ref, normed_ref,
):
    frames, rows = stream_ref.shape[:2]
    band = lax.axis_index("rows")
    keep_above = jnp.where(band > 0, 1.0, 0.0)
    keep_below = jnp.where(band < lax.axis_size("rows") - 1, 1.0, 0.0)
    odd = band % 2 == 1
    gain = gain_ref[0]

    activate_rows(
        taps_ref,
        frames,
        odd,
        lambda frame, row: stream_ref[frame, row],
        partner_ref,
        lambda frame, row, _: across_ref[frame, row],
        gain,
    )
    gain = gain_ref[1]
    bias = jnp.concatenate([bias_ref[0]] * 2, axis=1)
    for pair in range((rows + 2) // 2):
        y = [
            tap_products(weights_ref, 0, taps, row_pair(taps_ref, frame, 2 * pair))
            for frame, taps in enumerate(((0, 2), (0, 2), (1, 2), (2, 2)))
        ]
        hidden = [
            y[0][2] + bias,
            y[0][1] + y[1][2] + bias,
            y[0][0] + y[1][1] + y[2][2] + bias,
            y[1][0] + y[2][1] + y[3][2] + bias,
        ]
        for frame in range(4):
            for side, values in enumerate(halves(hidden[frame])):
                row = 2 * pair + side
                if frame < 2:
                    hidden_ref[frame, row] = values
                    continue
                act = activated(values, gain)
                if row == 0:
                    act = act * keep_above
                if row == rows + 1:
                    act = act * keep_below
                store_taps(normed_ref, frame - 2, row, act)
    bias = bias_ref[1]
    for pair in range(rows // 2):
        y2 = tap_products(weights_ref, 1, (0, 2), row_pair(normed_ref, 0, 2 * pair))
        y3 = tap_products(weights_ref, 1, (0, 2), row_pair(normed_ref, 1, 2 * pair))
        for side in range(2):
            row = 2 * pair + side
            send_ref[0, row] = (halves(y2[0])[side] + halves(y3[1])[side]).astype(BF16)
            send_ref[1, row] = halves(y3[0])[side].astype(BF16)
            base_ref[0, row] = halves(y2[2])[side] + bias + stream_ref[2, row].astype(F32)
            base_ref[1, row] = (
                halves(y2[1])[side] + halves(y3[2])[side] + bias + stream_ref[3, row].astype(F32)
            )


def history_kernel(
    earlier_ref, narrow_ref, rest_ref, corner_ref, partner_ref, hidden_ref, base_ref, stream_ref, weights_ref, gain_ref, bias_ref,
    out_ref, first_ref,
    taps_ref, normed_ref,
):
    rows = earlier_ref.shape[1]
    band = lax.axis_index("rows")
    keep_above = jnp.where(band > 0, 1.0, 0.0)
    keep_below = jnp.where(band < lax.axis_size("rows") - 1, 1.0, 0.0)
    odd = band % 2 == 1
    gain = gain_ref[0]

    relay, swap = first_block_bands()

    def own(frame, row):
        half = narrow_ref.shape[1]
        relayed = narrow_ref[frame, row] if row < half else rest_ref[frame, row - half]
        return jnp.where(relay, relayed, earlier_ref[frame, row])

    def across(frame, row, start):
        swapped = narrow_ref[frame, row + (narrow_ref.shape[1] - 2 if start == 0 else 0)]
        return jnp.where(swap, swapped, corner_ref[frame, row])

    activate_rows(
        taps_ref,
        2,
        odd,
        own,
        partner_ref,
        across,
        gain,
    )
    gain = gain_ref[1]
    for pair in range((rows + 2) // 2):
        y0 = tap_products(weights_ref, 0, (0, 0), row_pair(taps_ref, 0, 2 * pair))
        y1 = tap_products(weights_ref, 0, (0, 1), row_pair(taps_ref, 1, 2 * pair))
        hidden = [y0[0] + y1[1], y1[0]]
        for frame in range(2):
            for side, values in enumerate(halves(hidden[frame])):
                row = 2 * pair + side
                act = activated(values + hidden_ref[frame, row], gain)
                if row == 0:
                    act = act * keep_above
                if row == rows + 1:
                    act = act * keep_below
                store_taps(normed_ref, frame, row, act)
    bias = bias_ref[1]
    for pair in range(rows // 2):
        y0 = tap_products(weights_ref, 1, (0, 2), row_pair(normed_ref, 0, 2 * pair))
        y1 = tap_products(weights_ref, 1, (0, 2), row_pair(normed_ref, 1, 2 * pair))
        for side in range(2):
            row = 2 * pair + side
            first_ref[0, row] = halves(y0[2])[side] + bias + stream_ref[0, row].astype(F32)
            first_ref[1, row] = (
                halves(y0[1])[side] + halves(y1[2])[side] + bias + stream_ref[1, row].astype(F32)
            )
            out_ref[2, row] = (
                base_ref[0, row] + halves(y0[0])[side] + halves(y1[1])[side]
            ).astype(BF16)
            out_ref[3, row] = (base_ref[1, row] + halves(y1[0])[side]).astype(BF16)


def finish_kernel(partial_ref, first_ref, _, out_ref):
    out_ref[...] = (first_ref[...] + partial_ref[...].astype(F32)).astype(BF16)


def call(kernel, outs, scratch=(), flops=0, moved=0):
    return pl.pallas_call(
        kernel,
        out_shape=[jax.ShapeDtypeStruct(*out) for out in outs],
        scratch_shapes=list(scratch),
        compiler_params=pltpu.CompilerParams(vmem_limit_bytes=VMEM_BYTES),
        cost_estimate=pl.CostEstimate(flops=flops, bytes_accessed=moved, transcendentals=0),
    )


def span(axis):
    return lax.axis_size(axis) // 4


def steps(axis, distance):
    size = lax.axis_size(axis)
    return [(i, i + distance) for i in range(size) if 0 <= i + distance < size]


def spread(pairs, bands):
    size = lax.axis_size("rows")
    return [(i * size + source, j * size + target) for i, j in pairs for source, target in bands]


def partners(block):
    return lax.ppermute(block, "rows", [(0, 1), (1, 0), (2, 3), (3, 2)])


def shards(stream, gains, kernels, biases):
    frames, rows, channels, cols = stream.shape
    plane = (channels, cols)
    cells = rows * cols
    mac = 2 * 9 * channels * channels
    edges = jax.ShapeDtypeStruct((frames, 2, *plane), BF16)
    recent, upper, lower = pl.pallas_call(
        cut_kernel,
        out_shape=[jax.ShapeDtypeStruct((2, rows, *plane), BF16), edges, edges],
        in_specs=[pl.BlockSpec(memory_space=pltpu.HBM)],
        scratch_shapes=[pltpu.SemaphoreType.DMA((3,))],
        compiler_params=pltpu.CompilerParams(vmem_limit_bytes=4 * 1024 * 1024),
    )(stream)
    following = steps("tm", 1)
    across = lax.ppermute(upper, "rows", [(1, 2), (2, 1)])
    mesh_axes = ("tm", "rows")
    outer_bands, inner_bands = [(0, 0), (3, 3)], [(1, 1), (2, 2)]
    size, group = lax.axis_size("tm"), span("tm")
    onward = [(i, i + group) for i in range(0, size - group, group)]
    crossing = [(i, j) for i, j in following if j % group == 0]
    straight = [(i, j) for i, j in following if j % group]
    turned = [(i, j - group) for i, j in crossing]
    first_blocks = [(j, j) for _, j in crossing]
    earlier = lax.ppermute(
        recent,
        mesh_axes,
        spread(straight, outer_bands + inner_bands)
        + spread(turned, outer_bands)
        + spread(crossing, inner_bands),
    )
    partner = partners(lower)
    taps = kernels.reshape(2, 3, 9 * channels, channels)
    weights, gain, bias = pl.pallas_call(
        prepare_kernel,
        out_shape=[
            jax.ShapeDtypeStruct((2, 3 * channels, 9 * channels), BF16),
            jax.ShapeDtypeStruct((2, *plane), F32),
            jax.ShapeDtypeStruct((2, *plane), F32),
        ],
        in_specs=[pl.BlockSpec(memory_space=pltpu.HBM)] * 3,
        scratch_shapes=[
            pltpu.VMEM(taps.shape, BF16),
            pltpu.VMEM(gains.shape, F32),
            pltpu.VMEM(biases.shape, F32),
            pltpu.SemaphoreType.DMA((3,)),
        ],
        compiler_params=pltpu.CompilerParams(vmem_limit_bytes=VMEM_BYTES),
        cost_estimate=pl.CostEstimate(flops=10**6, bytes_accessed=0, transcendentals=0),
    )(taps, gains, biases)
    sent, hidden, base = call(
        local_kernel,
        [
            ((2, rows, *plane), BF16),
            ((2, rows + 2, *plane), F32),
            ((2, rows, *plane), F32),
        ],
        [
            pltpu.VMEM((frames, rows + 4, 3 * channels, cols), BF16),
            pltpu.VMEM((2, rows + 2, 3 * channels, cols), BF16),
        ],
        flops=0,
        moved=0,
    )(stream, partner, across, weights, gain, bias)
    partial = lax.ppermute(sent, "tm", following)
    corner, sent = lax.optimization_barrier((across[frames - 2 :], sent))
    corner = lax.ppermute(corner, mesh_axes, spread(straight, inner_bands))
    earlier, sent = lax.optimization_barrier((earlier, sent))
    half = rows // 2 - 1
    (narrow,) = call(narrow_kernel, [((2, half, *plane), BF16)])(earlier)
    narrow = lax.ppermute(
        narrow, mesh_axes, spread(onward, outer_bands) + spread(first_blocks, [(1, 2), (2, 1)])
    )
    rest = lax.ppermute(earlier[:, half:], mesh_axes, spread(onward, outer_bands))
    (edge,) = call(edge_kernel, [((2, 2, *plane), BF16)])(earlier, narrow, rest)
    beside = partners(edge)
    out, first = call(
        history_kernel,
        [((frames, rows, *plane), BF16), ((2, rows, *plane), F32)],
        [
            pltpu.VMEM((2, rows + 4, 3 * channels, cols), BF16),
            pltpu.VMEM((2, rows + 2, 3 * channels, cols), BF16),
        ],
        flops=0,
        moved=0,
    )(earlier, narrow, rest, corner, beside, hidden, base, stream, weights, gain, bias)
    block = pl.BlockSpec((2, rows, *plane), lambda i: (0, 0, 0, 0))
    return pl.pallas_call(
        finish_kernel,
        grid=(1,),
        out_shape=jax.ShapeDtypeStruct(stream.shape, BF16),
        in_specs=[block, block, pl.BlockSpec(memory_space=pl.ANY)],
        out_specs=block,
        input_output_aliases={2: 0},
        compiler_params=pltpu.CompilerParams(vmem_limit_bytes=VMEM_BYTES),
        cost_estimate=pl.CostEstimate(flops=10**6, bytes_accessed=2 * 10**6, transcendentals=0),
    )(partial, first, out)


def solution(mesh):
    placed = (P("tm", "rows", None, None), P(), P(), P())
    return jax.shard_map(
        shards, mesh=mesh, in_specs=placed, out_specs=P("tm", "rows", None, None), check_vma=False
    )
```
